32 devices in a mesh: circ: 4 (over y, x), span: 8 (over z, core).
Axes of the slice: x: 2, y: 2, z: 4, core: 2. Of those that a mesh axis runs over, the one named last changes fastest.
Arguments:
- q_old: float32 [5, 16, 1024, 128], P(None, 'circ', 'span'), may hold values from -6 to 6
- pseudo_rate: float32 [16, 1024, 128], P('circ', 'span'), may hold values from 0.15 to 0.45
- flux_jacobians: float32 [3, 5, 5], replicated, may hold values from -2.5 to 2.5
- rotor_face: float32 [5, 16, 1024], P(None, 'circ', 'span'), may hold values from -6 to 6
- offsets: int32 [1024], P('span'), may hold values from 0 to 15
- owners: int32 [4, 32, 4], P('circ', 'span'), may hold values from 0 to 7, all different within a row; in each aligned block of 4 rows (0 to 3, 4 to 7, ..., all dimensions but the last counted through in order) at most 4 rows name the same one
- slots: int32 [4, 32, 4], P('circ', 'span'), may hold values from 0 to 3
- weight_idx: int32 [4, 32, 4], P('circ', 'span'), may hold values from 0 to 15
- weight_table: float32 [16], replicated, may hold values from 0.3 to 1
Outputs:
- q_new: float32 [5, 16, 1024, 128], P(None, 'circ', 'span')
The draws below stay inside these ranges and needn't reach their ends.
Inputs may be any that keep to these rules, and one draw needn't show every extreme that they name: The 4 owners of one rotor panel differ; among the 4 rotor panels of one device in one circumferential block, no owner is named more than 4 times, and that count is reached.
All inputs are finite; a program needn't handle non-finite values.
Results may differ from the reference program's by a relative error of at most 0.000068.
Values sent between devices are 32-bit elements; how exact they have to be, the bound alone decides.
A program may use at most 64 MiB of HBM per device.

```python
import math
import jax
import jax.numpy as jnp
import numpy as np
from jax import lax

NF = 5
CT = 4
KP_DEV = 4
PW = 32
TOP = 4
NW = 16
CA = 128
CAP = 4
NB = 4
NT = 16
NS = 1024
KP = 32
N_SPAN = 8


def with_ends(drawn, stream_key, least, largest):
    longest = drawn.shape.index(max(drawn.shape))
    spots = []
    for shift in (0, 1):
        where = [jax.random.randint(jax.random.fold_in(stream_key, axis), (), 0, length) for axis, length in enumerate(drawn.shape)]
        where[longest] = (where[longest] + shift) % drawn.shape[longest]
        spots.append(tuple(where))
    return drawn.at[spots[0]].set(least).at[spots[1]].set(largest)


def block_scale(stream_key, extent, pieces, least, high):
    def one(dim, shards_of):
        heights = jax.random.uniform(jax.random.fold_in(jax.random.fold_in(stream_key, 6), dim), (shards_of,), jnp.float32, least / len(pieces), high / len(pieces))
        return jnp.repeat(jnp.exp(heights), extent[dim] // shards_of).reshape((-1,) + (1,) * (len(extent) - dim - 1))

    loudness = one(*pieces[0])
    for cut in pieces[1:]:
        loudness = loudness * one(*cut)
    return loudness


def shared_out(key, own, number, rows, count, top, limit, lean):
    order = jax.random.permutation(key, count)
    packed, usual = portions_of(count, rows * top, limit, lean, True), portions_of(count, rows * top, limit, lean, False)
    places = jnp.arange(count)

    def named(lengths, offset_by):
        used = int((lengths > 0).sum())
        fixed = max(1, used // 4)
        shifted = fixed + (places - fixed + offset_by * (used - fixed)) % max(1, count - fixed)
        return jnp.zeros((count,), jnp.int32).at[order[jnp.where(places < fixed, places, shifted)]].set(jnp.asarray(lengths, jnp.int32))

    lengths = jnp.where(number % 4 == 0, named(packed, number // 4), named(usual, number - number // 4 - 1))
    mixed = jax.random.permutation(jax.random.fold_in(own, 3), count)
    giver, receiver = mixed[0:count // 2 * 2:2], mixed[1:count // 2 * 2:2]
    slack = jnp.minimum(lengths[giver] - 1, limit - lengths[receiver]) // 2
    slack = jnp.where((giver == order[0]) | (receiver == order[0]) | (lengths[receiver] == 0), 0, jnp.maximum(slack, 0))
    shifted = jax.random.randint(jax.random.fold_in(own, 4), (count // 2,), 0, 1 << 20) % (slack + 1)
    lengths = lengths.at[giver].add(-shifted).at[receiver].add(shifted)
    items = jnp.searchsorted(jnp.cumsum(lengths), jnp.arange(rows * top), side="right").astype(jnp.int32)
    table = items.reshape(top, rows).T
    table = table[jax.random.permutation(jax.random.fold_in(own, 1), rows)]
    offset_by = jax.random.randint(jax.random.fold_in(own, 2), (rows, 1), 0, top)
    return jnp.take_along_axis(table, (jnp.arange(top)[None, :] + offset_by) % top, axis=1)


def portions_of(count, total, limit, lean, full):
    loads = [(1 << 20) // math.isqrt(grade ** lean) + 1 for grade in range(1, count + 1)]
    largest = limit if full else min(limit, max(-(-total // count), total * loads[0] // sum(loads)))
    least = 1 if total - largest >= count - 1 else 0
    counts, spare = [largest] + [least] * (count - 1), total - largest - least * (count - 1)
    while spare > 0:
        free = [i for i in range(1, count) if counts[i] < largest] or [i for i in range(1, count) if counts[i] < limit]
        pool, left = sum([loads[i] for i in free]), spare
        for i in free:
            extra = min(limit - counts[i], max(1, left * loads[i] // pool), spare)
            counts[i] = counts[i] + extra
            spare = spare - extra
    return np.array(counts)


def centred(rng, extent, deviation, bound, cuts=(), kind=jnp.bfloat16):
    entries = deviation * jax.random.normal(rng, extent, jnp.float32)
    if cuts:
        entries = entries * block_scale(rng, extent, cuts, -0.22, 0.18)
    return jnp.clip(entries, -bound, bound).astype(kind)


def setup_inputs(seed: int = 0) -> dict:
    key_list = jax.random.split(jax.random.key(seed), 10)
    q_old = centred(key_list[0], (NF, NT, NS, CA), 1.0, 6.0, ((1, 4), (2, 8)), jnp.float32)
    pseudo_rate = jnp.clip(jnp.exp(math.log(0.45) - 1.0986122 * jax.random.uniform(key_list[1], (NT, NS, CA), jnp.float32) ** block_scale(key_list[1], (NT, NS, CA), ((0, 4), (1, 8)), -0.2, 0.2)), 0.15, 0.45)
    flux_jacobians = centred(key_list[2], (3, NF, NF), NF ** -0.5, 2.5, (), jnp.float32)
    rotor_face = centred(key_list[3], (NF, NT, NS), 1.0, 6.0, ((1, 4), (2, 8)), jnp.float32)
    offsets = with_ends(jax.random.randint(key_list[4], (NS,), 0, NT), jax.random.fold_in(key_list[4], 1), 0, NT - 1).astype(jnp.int32)
    owners_keys = jax.random.split(jax.random.fold_in(key_list[5], 1), NB * KP // KP_DEV)
    owners_turns = jax.random.permutation(jax.random.fold_in(key_list[5], 3), NB * KP // KP_DEV)
    owners = jax.vmap(lambda own, number: shared_out(jax.random.fold_in(key_list[5], 2), own, number, KP_DEV, N_SPAN, TOP, CAP, 2))(owners_keys, owners_turns).reshape((NB, KP, TOP))
    slots = with_ends(jax.random.randint(key_list[6], (NB, KP, TOP), 0, KP_DEV), jax.random.fold_in(key_list[6], 1), 0, KP_DEV - 1).astype(jnp.int32)
    weight_idx = with_ends(jax.random.randint(key_list[7], (NB, KP, TOP), 0, NW), jax.random.fold_in(key_list[7], 1), 0, NW - 1).astype(jnp.int32)
    weight_table = jnp.clip(jax.random.uniform(key_list[8], (NW,), jnp.float32, 0.3, 1.0), 0.3, 1.0)
    return {"q_old": q_old, "pseudo_rate": pseudo_rate, "flux_jacobians": flux_jacobians, "rotor_face": rotor_face, "offsets": offsets, "owners": owners, "slots": slots, "weight_idx": weight_idx, "weight_table": weight_table}


inv_step = 0.5
viscosity = 0.1


def contract(matrix, values):
    return jnp.einsum("fg,gtsa->ftsa", matrix, values, precision=lax.Precision.HIGHEST)


def advance(padded, current, previous, rate_cells, inlet_plane, jacobians):
    circ_up = padded[:, 2:, 1:-1]
    circ_down = padded[:, :-2, 1:-1]
    span_up = padded[:, 1:-1, 2:]
    span_down = padded[:, 1:-1, :-2]
    zero_column = jnp.zeros_like(current[..., :1])
    axial_up = jnp.concatenate([current[..., 1:], zero_column], axis=-1)
    axial_down = jnp.concatenate([inlet_plane[..., None], current[..., :-1]], axis=-1)
    convection = contract(jacobians[0], circ_up - circ_down)
    convection = convection + contract(jacobians[1], span_up - span_down)
    convection = convection + contract(jacobians[2], axial_up - axial_down)
    laplacian = (circ_up + circ_down) + (span_up + span_down) + (axial_up + axial_down) - 6.0 * current
    residual = inv_step * (current - previous) + 0.5 * convection - viscosity * laplacian
    return current - rate_cells[None] * residual


def extend(field_values):
    wrapped = jnp.concatenate([field_values[:, -1:], field_values, field_values[:, :1]], axis=1)
    return jnp.pad(wrapped, ((0, 0), (0, 0), (1, 1), (0, 0)))


def reference(q_old, pseudo_rate, flux_jacobians, rotor_face, offsets, owners, slots, weight_idx, weight_table):
    source_rows = (jnp.arange(NT, dtype=jnp.int32)[:, None] - offsets[None, :]) % NT
    rotated = jnp.take_along_axis(rotor_face, source_rows[None].astype(jnp.int32), axis=1)
    panels = rotated.reshape(NF, NB, CT, KP, PW)
    weights = weight_table[weight_idx]
    targets = owners * KP_DEV + slots
    panel_ids = jnp.arange(KP, dtype=jnp.int32)
    mixing = jnp.sum(jnp.where(targets[:, None, :, :] == panel_ids[None, :, None, None], weights[:, None, :, :], 0.0), axis=-1)
    inlet_plane = jnp.einsum("cgk,fctkp->fctgp", mixing, panels, precision=lax.Precision.HIGHEST).reshape(NF, NT, NS)
    first_pass = advance(extend(q_old), q_old, q_old, pseudo_rate, inlet_plane, flux_jacobians)
    return advance(extend(first_pass), first_pass, q_old, pseudo_rate, inlet_plane, flux_jacobians)
```

```python
import functools

import jax
import jax.numpy as jnp
from jax import lax
from jax.experimental import pallas as pl
from jax.experimental.pallas import tpu as pltpu
from jax.sharding import PartitionSpec as P

NF = 5
CT = 4
PANELS = 4
ROWS = 16
CHUNKS = 4
PAD = 8

inv_step = 0.5
viscosity = 0.1


def remote(src, dst, send, recv, **device):
    return pltpu.make_async_remote_copy(
        src_ref=src,
        dst_ref=dst,
        send_sem=send,
        recv_sem=recv,
        device_id=device,
        device_id_type=pl.DeviceIdType.MESH,
    )


def kernel(
    n_circ, n_span,
    q_hbm, rate_hbm, jac, rotor, offsets, owners, slots, weight_idx, table,
    out_hbm,
    q0, q1, rate, out, ends, halo0, halo1,
    rotor_in, given, taken, inlet_rows, inlet_cols, span_out, span_in,
    local_sem, out_sem, rotor_s, rotor_r, panel_s, panel_r,
    circ_s, circ_r, span_s, span_r,
):
    span_len = q_hbm.shape[2]
    cells = q_hbm.shape[3]
    step = span_len // CHUNKS
    total = n_circ * CT
    me_c = lax.axis_index("circ")
    me_s = lax.axis_index("span")

    load_q = pltpu.make_async_copy(q_hbm, q0.at[:, :, pl.ds(PAD, span_len)], local_sem.at[0])
    load_q.start()
    load_rate = pltpu.make_async_copy(rate_hbm, rate, local_sem.at[1])
    load_rate.start()

    barrier = pltpu.get_barrier_semaphore()
    for off in range(1, n_circ):
        pl.semaphore_signal(
            barrier, inc=1, device_id={"circ": lax.rem(me_c + off, n_circ)},
            device_id_type=pl.DeviceIdType.MESH,
        )
    for off in range(1, n_span):
        pl.semaphore_signal(
            barrier, inc=1, device_id={"span": lax.rem(me_s + off, n_span)},
            device_id_type=pl.DeviceIdType.MESH,
        )
    pl.semaphore_wait(barrier, n_circ - 1 + n_span - 1)

    up_c = lax.rem(me_c + 1, n_circ)
    down_c = lax.rem(me_c + n_circ - 1, n_circ)

    rotor_copies = []
    for off in range(1, n_circ):
        copy = remote(
            rotor, rotor_in.at[off - 1], rotor_s.at[off - 1], rotor_r.at[off - 1],
            circ=lax.rem(me_c + off, n_circ),
        )
        copy.start()
        rotor_copies.append(copy)

    def circ_copy(phase, chunk, side):
        part = pl.ds(chunk * step, step)
        row = CT - 1 if side == 0 else 0
        if phase == 0:
            src = q_hbm.at[:, row, part]
            dst = halo0.at[side, :, part]
        else:
            src = q1.at[:, row, pl.ds(PAD + chunk * step, step)]
            dst = halo1.at[side, :, part]
        return remote(
            src, dst, circ_s.at[phase, chunk, side], circ_r.at[phase, chunk, side],
            circ=up_c if side == 0 else down_c,
        )

    for chunk in range(CHUNKS):
        for side in range(2):
            circ_copy(0, chunk, side).start()

    def span_copy(phase, side):
        return remote(
            span_out.at[phase, side], span_in.at[phase, side],
            span_s.at[phase, side], span_r.at[phase, side],
            span=lax.rem(me_s + (1 if side == 0 else n_span - 1), n_span),
        )

    def span_send(phase, q):
        for f in range(NF):
            for t in range(CT):
                span_out[phase, 0, f, pl.ds(t, 1)] = q[f, t, pl.ds(PAD + span_len - 1, 1)]
                span_out[phase, 1, f, pl.ds(t, 1)] = q[f, t, pl.ds(PAD, 1)]

        @pl.when(me_s < n_span - 1)
        def _():
            span_copy(phase, 0).start()

        @pl.when(me_s > 0)
        def _():
            span_copy(phase, 1).start()

    def span_take(phase, q):
        @pl.when(me_s > 0)
        def _():
            span_copy(phase, 0).wait_recv()

        @pl.when(me_s == 0)
        def _():
            span_in[phase, 0] = jnp.zeros((NF, CT, cells), jnp.float32)

        @pl.when(me_s < n_span - 1)
        def _():
            span_copy(phase, 1).wait_recv()

        @pl.when(me_s == n_span - 1)
        def _():
            span_in[phase, 1] = jnp.zeros((NF, CT, cells), jnp.float32)

        for f in range(NF):
            for t in range(CT):
                q[f, t, pl.ds(PAD - 1, 1)] = span_in[phase, 0, f, pl.ds(t, 1)]
                q[f, t, pl.ds(PAD + span_len, 1)] = span_in[phase, 1, f, pl.ds(t, 1)]

    load_q.wait()
    span_send(0, q0)

    lane = lax.broadcasted_iota(jnp.int32, (CT, span_len), 1)
    quarter = lane // (span_len // PANELS)
    width = span_len // PANELS
    turned = lax.broadcasted_iota(jnp.int32, (CT, span_len), 0) - offsets[...]
    turned = jnp.where(turned < 0, turned + total, turned)
    spot = (
        lax.broadcasted_iota(jnp.int32, (n_span, span_len), 0) * PANELS
        + lax.broadcasted_iota(jnp.int32, (n_span, span_len), 1) // width
    )
    mixing = []
    for k in range(PANELS):
        mix = jnp.zeros((n_span, span_len), jnp.float32)
        for j in range(owners.shape[2]):
            weight = table[weight_idx[0, k, j]]
            mix = mix + jnp.where(spot == owners[0, k, j] * PANELS + slots[0, k, j], weight, 0.0)
        mixing.append(mix)

    for copy in rotor_copies:
        copy.wait_recv()
    for f in range(NF):
        rotated = jnp.zeros((CT, span_len), jnp.float32)
        for off in range(n_circ):
            for i in range(CT):
                row = rotor[f, pl.ds(i, 1)] if off == 0 else rotor_in[off - 1, f, pl.ds(i, 1)]
                rotated = jnp.where(turned == (i - CT * off) % total, row, rotated)
        rolled = [rotated] + [pltpu.roll(rotated, width * d, 1) for d in range(1, PANELS)]
        tiled = []
        for k in range(PANELS):
            value = rolled[(0 - k) % PANELS]
            for b in range(1, PANELS):
                value = jnp.where(quarter == b, rolled[(b - k) % PANELS], value)
            tiled.append(value)
        for o in range(n_span):
            value = mixing[0][o:o + 1] * tiled[0]
            for k in range(1, PANELS):
                value = value + mixing[k][o:o + 1] * tiled[k]
            given[o, f] = value

    panel_copies = []
    for off in range(1, n_span):
        peer = lax.rem(me_s + off, n_span)
        copy = remote(
            given.at[peer], taken.at[off - 1], panel_s.at[off - 1], panel_r.at[off - 1], span=peer
        )
        copy.start()
        panel_copies.append(copy)
    inlet_rows[...] = jnp.zeros(inlet_rows.shape, jnp.float32)
    load_rate.wait()
    span_take(0, q0)
    for copy in panel_copies:
        copy.wait_recv()
    for f in range(NF):
        value = given[me_s, f]
        for off in range(1, n_span):
            value = value + taken[off - 1, f]
        inlet_rows[pl.ds(f * CT, CT)] = value
    inlet_cols[...] = inlet_rows[...].T

    def spread(i, carry):
        part = pl.ds(pl.multiple_of(i * 8, 8), 8)
        columns = inlet_cols[part]
        for f in range(NF):
            for t in range(CT):
                shift = (-(f * CT + t)) % cells
                ends[f, t, part] = pltpu.roll(columns, shift, 1) if shift else columns
        return carry

    lax.fori_loop(0, span_len // 8, spread, 0)

    coefs = [[[inv_step * jac[d, f, g] for g in range(NF)] for f in range(NF)] for d in range(3)]
    axial = lax.broadcasted_iota(jnp.int32, (ROWS, cells), 1)
    at_first = axial == 0
    at_last = axial == cells - 1

    def advance(q, halo, target, pad, t, s, first):
        part = pl.ds(pl.multiple_of(PAD + s, 8), ROWS)
        plain = pl.ds(pl.multiple_of(s, 8), ROWS)
        now, diffs, sums = [], [], []
        for g in range(NF):
            c = q[g, t, part]
            if isinstance(t, int) and t == CT - 1:
                cu = halo[1, g, plain]
            else:
                cu = q[g, t + 1, part]
            if isinstance(t, int) and t == 0:
                cd = halo[0, g, plain]
            else:
                cd = q[g, t - 1, part]
            su = q[g, t, pl.ds(PAD + 1 + s, ROWS)]
            sd = q[g, t, pl.ds(PAD - 1 + s, ROWS)]
            au = jnp.where(at_last, 0.0, pltpu.roll(c, cells - 1, 1))
            ad = jnp.where(at_first, ends[g, t, plain], pltpu.roll(c, 1, 1))
            now.append(c)
            diffs.append((cu - cd, su - sd, au - ad))
            sums.append((cu + cd) + (su + sd) + (au + ad))
        speed = rate[t, plain]
        for f in range(NF):
            residual = (6.0 * now[f] - sums[f]) * viscosity
            if not first:
                residual = residual + inv_step * (now[f] - q0[f, t, part])
            for d in range(3):
                for g in range(NF):
                    residual = residual + coefs[d][f][g] * diffs[g][d]
            target[f, t, part if pad else plain] = now[f] - speed * residual

    per_chunk = step // ROWS

    def edges(q, halo, target, pad, chunk, first):
        def one(i, carry):
            s = chunk * step + i * ROWS
            advance(q, halo, target, pad, 0, s, first)
            advance(q, halo, target, pad, CT - 1, s, first)
            return carry

        lax.fori_loop(0, per_chunk, one, 0)

    def inner(q, target, pad, first):
        def one(i, carry):
            t = 1 + i // (span_len // ROWS)
            advance(q, None, target, pad, t, i % (span_len // ROWS) * ROWS, first)
            return carry

        lax.fori_loop(0, (CT - 2) * (span_len // ROWS), one, 0)

    for chunk in range(CHUNKS):
        for side in range(2):
            circ_copy(0, chunk, side).wait_recv()
        edges(q0, halo0, q1, True, chunk, True)
        for side in range(2):
            circ_copy(1, chunk, side).start()
    inner(q0, q1, True, True)
    span_send(1, q1)
    span_take(1, q1)
    inner(q1, out, False, False)
    store = pltpu.make_async_copy(
        out.at[:, pl.ds(1, CT - 2)], out_hbm.at[:, pl.ds(1, CT - 2)], out_sem.at[0]
    )
    store.start()
    stores = [store]
    for chunk in range(CHUNKS):
        for side in range(2):
            circ_copy(1, chunk, side).wait_recv()
        edges(q1, halo1, out, False, chunk, False)
        part = pl.ds(chunk * step, step)
        for side, row in enumerate((0, CT - 1)):
            store = pltpu.make_async_copy(
                out.at[:, row, part], out_hbm.at[:, row, part], out_sem.at[1 + 2 * chunk + side]
            )
            store.start()
            stores.append(store)

    for copy in rotor_copies + panel_copies:
        copy.wait_send()
    for phase in range(2):
        for chunk in range(CHUNKS):
            for side in range(2):
                circ_copy(phase, chunk, side).wait_send()

        @pl.when(me_s < n_span - 1)
        def _():
            span_copy(phase, 0).wait_send()

        @pl.when(me_s > 0)
        def _():
            span_copy(phase, 1).wait_send()
    for store in stores:
        store.wait()


def body(
    n_circ, n_span,
    q_old, pseudo_rate, flux_jacobians, rotor_face, offsets, owners, slots, weight_idx, weight_table,
):
    nf, ct, span_len, cells = q_old.shape
    f32 = jnp.float32
    hbm = pl.BlockSpec(memory_space=pl.ANY)
    vmem = pl.BlockSpec(memory_space=pltpu.VMEM)
    smem = pl.BlockSpec(memory_space=pltpu.SMEM)
    dma = pltpu.SemaphoreType.DMA
    padded = pltpu.VMEM((nf, ct, span_len + 2 * PAD, cells), f32)
    block = pltpu.VMEM((nf, ct, span_len, cells), f32)
    halo = pltpu.VMEM((2, nf, span_len, cells), f32)
    return pl.pallas_call(
        functools.partial(kernel, n_circ, n_span),
        out_shape=jax.ShapeDtypeStruct(q_old.shape, f32),
        in_specs=[hbm, hbm, smem, vmem, vmem, smem, smem, smem, smem],
        out_specs=hbm,
        scratch_shapes=[
            padded, padded, pltpu.VMEM((ct, span_len, cells), f32), block, block, halo, halo,
            pltpu.VMEM((n_circ - 1, nf, ct, span_len), f32),
            pltpu.VMEM((n_span, nf, ct, span_len), f32),
            pltpu.VMEM((n_span - 1, nf, ct, span_len), f32),
            pltpu.VMEM((cells, span_len), f32),
            pltpu.VMEM((span_len, cells), f32),
            pltpu.VMEM((2, 2, nf, ct, cells), f32),
            pltpu.VMEM((2, 2, nf, ct, cells), f32),
            dma((2,)), dma((1 + 2 * CHUNKS,)),
            dma((n_circ - 1,)), dma((n_circ - 1,)),
            dma((n_span - 1,)), dma((n_span - 1,)),
            dma((2, CHUNKS, 2)), dma((2, CHUNKS, 2)),
            dma((2, 2)), dma((2, 2)),
        ],
        compiler_params=pltpu.CompilerParams(
            collective_id=0, has_side_effects=True, vmem_limit_bytes=40 * 1024 * 1024
        ),
    )(
        q_old, pseudo_rate, flux_jacobians, rotor_face, offsets.reshape(1, span_len),
        owners, slots, weight_idx, weight_table,
    )


def solution(mesh):
    return jax.shard_map(
        functools.partial(body, mesh.shape["circ"], mesh.shape["span"]),
        mesh=mesh,
        in_specs=(
            P(None, "circ", "span", None),
            P("circ", "span", None),
            P(),
            P(None, "circ", "span"),
            P("span"),
            P("circ", "span", None),
            P("circ", "span", None),
            P("circ", "span", None),
            P(),
        ),
        out_specs=P(None, "circ", "span", None),
        check_vma=False,
    )
```

```python
import functools

import jax
import jax.numpy as jnp
from jax import lax
from jax.experimental import pallas as pl
from jax.experimental.pallas import tpu as pltpu
from jax.sharding import PartitionSpec as P

NF = 5
CT = 4
PANELS = 4
ROWS = 32
CHUNKS = 4
PAD = 8

inv_step = 0.5
viscosity = 0.1


def remote(src, dst, send, recv, **device):
    return pltpu.make_async_remote_copy(
        src_ref=src,
        dst_ref=dst,
        send_sem=send,
        recv_sem=recv,
        device_id=device,
        device_id_type=pl.DeviceIdType.MESH,
    )


def kernel(
    n_circ, n_span,
    q_hbm, rate_hbm, jac, rotor, offsets, owners, slots, weight_idx, table,
    out,
    q0, q1, rate, ends, halo0, halo1,
    rotor_in, given, taken, inlet_rows, inlet_cols, span_out, span_in,
    local_sem, rotor_s, rotor_r, panel_s, panel_r,
    circ_s, circ_r, span_s, span_r,
):
    span_len = q_hbm.shape[2]
    cells = q_hbm.shape[3]
    step = span_len // CHUNKS
    total = n_circ * CT
    me_c = lax.axis_index("circ")
    me_s = lax.axis_index("span")

    load_q = pltpu.make_async_copy(q_hbm, q0.at[:, :, pl.ds(PAD, span_len)], local_sem.at[0])
    load_q.start()
    load_rate = pltpu.make_async_copy(rate_hbm, rate, local_sem.at[1])
    load_rate.start()

    barrier = pltpu.get_barrier_semaphore()
    for off in range(1, n_circ):
        pl.semaphore_signal(
            barrier, inc=1, device_id={"circ": lax.rem(me_c + off, n_circ)},
            device_id_type=pl.DeviceIdType.MESH,
        )
    for off in range(1, n_span):
        pl.semaphore_signal(
            barrier, inc=1, device_id={"span": lax.rem(me_s + off, n_span)},
            device_id_type=pl.DeviceIdType.MESH,
        )
    pl.semaphore_wait(barrier, n_circ - 1 + n_span - 1)

    up_c = lax.rem(me_c + 1, n_circ)
    down_c = lax.rem(me_c + n_circ - 1, n_circ)

    rotor_copies = []
    for off in range(1, n_circ):
        copy = remote(
            rotor, rotor_in.at[off - 1], rotor_s.at[off - 1], rotor_r.at[off - 1],
            circ=lax.rem(me_c + off, n_circ),
        )
        copy.start()
        rotor_copies.append(copy)

    def circ_copy(phase, chunk, side):
        part = pl.ds(chunk * step, step)
        row = CT - 1 if side == 0 else 0
        if phase == 0:
            src = q_hbm.at[:, row, part]
            dst = halo0.at[side, :, part]
        else:
            src = q1.at[:, row, pl.ds(PAD + chunk * step, step)]
            dst = halo1.at[side, :, part]
        return remote(
            src, dst, circ_s.at[phase, chunk, side], circ_r.at[phase, chunk, side],
            circ=up_c if side == 0 else down_c,
        )

    for chunk in range(CHUNKS // 4):
        for side in range(2):
            circ_copy(0, chunk, side).start()

    def span_copy(phase, side):
        return remote(
            span_out.at[phase, side], span_in.at[phase, side],
            span_s.at[phase, side], span_r.at[phase, side],
            span=lax.rem(me_s + (1 if side == 0 else n_span - 1), n_span),
        )

    def span_send(phase, q):
        for f in range(NF):
            for t in range(CT):
                span_out[phase, 0, f, pl.ds(t, 1)] = q[f, t, pl.ds(PAD + span_len - 1, 1)]
                span_out[phase, 1, f, pl.ds(t, 1)] = q[f, t, pl.ds(PAD, 1)]

        @pl.when(me_s < n_span - 1)
        def _():
            span_copy(phase, 0).start()

        @pl.when(me_s > 0)
        def _():
            span_copy(phase, 1).start()

    def span_take(phase, q):
        @pl.when(me_s > 0)
        def _():
            span_copy(phase, 0).wait_recv()

        @pl.when(me_s == 0)
        def _():
            span_in[phase, 0] = jnp.zeros((NF, CT, cells), jnp.float32)

        @pl.when(me_s < n_span - 1)
        def _():
            span_copy(phase, 1).wait_recv()

        @pl.when(me_s == n_span - 1)
        def _():
            span_in[phase, 1] = jnp.zeros((NF, CT, cells), jnp.float32)

        for f in range(NF):
            for t in range(CT):
                q[f, t, pl.ds(PAD - 1, 1)] = span_in[phase, 0, f, pl.ds(t, 1)]
                q[f, t, pl.ds(PAD + span_len, 1)] = span_in[phase, 1, f, pl.ds(t, 1)]

    load_q.wait()
    span_send(0, q0)

    lane = lax.broadcasted_iota(jnp.int32, (CT, span_len), 1)
    quarter = lane // (span_len // PANELS)
    width = span_len // PANELS
    turned = lax.broadcasted_iota(jnp.int32, (CT, span_len), 0) - offsets[...]
    turned = jnp.where(turned < 0, turned + total, turned)
    spot = (
        lax.broadcasted_iota(jnp.int32, (n_span, span_len), 0) * PANELS
        + lax.broadcasted_iota(jnp.int32, (n_span, span_len), 1) // width
    )
    mixing = []
    for k in range(PANELS):
        mix = jnp.zeros((n_span, span_len), jnp.float32)
        for j in range(owners.shape[2]):
            weight = table[weight_idx[0, k, j]]
            mix = mix + jnp.where(spot == owners[0, k, j] * PANELS + slots[0, k, j], weight, 0.0)
        mixing.append(mix)

    for copy in rotor_copies:
        copy.wait_recv()
    for f in range(NF):
        rotated = jnp.zeros((CT, span_len), jnp.float32)
        for off in range(n_circ):
            for i in range(CT):
                row = rotor[f, pl.ds(i, 1)] if off == 0 else rotor_in[off - 1, f, pl.ds(i, 1)]
                rotated = jnp.where(turned == (i - CT * off) % total, row, rotated)
        rolled = [rotated] + [pltpu.roll(rotated, width * d, 1) for d in range(1, PANELS)]
        tiled = []
        for k in range(PANELS):
            value = rolled[(0 - k) % PANELS]
            for b in range(1, PANELS):
                value = jnp.where(quarter == b, rolled[(b - k) % PANELS], value)
            tiled.append(value)
        for o in range(n_span):
            value = mixing[0][o:o + 1] * tiled[0]
            for k in range(1, PANELS):
                value = value + mixing[k][o:o + 1] * tiled[k]
            given[o, f] = value

    panel_copies = []
    for off in range(1, n_span):
        peer = lax.rem(me_s + off, n_span)
        copy = remote(
            given.at[peer], taken.at[off - 1], panel_s.at[off - 1], panel_r.at[off - 1], span=peer
        )
        copy.start()
        panel_copies.append(copy)
    for chunk in range(CHUNKS // 4, CHUNKS):
        for side in range(2):
            circ_copy(0, chunk, side).start()
    inlet_rows[...] = jnp.zeros(inlet_rows.shape, jnp.float32)
    load_rate.wait()
    span_take(0, q0)
    for copy in panel_copies:
        copy.wait_recv()
    for f in range(NF):
        value = given[me_s, f]
        for off in range(1, n_span):
            value = value + taken[off - 1, f]
        inlet_rows[pl.ds(f * CT, CT)] = value
    inlet_cols[...] = inlet_rows[...].T

    def spread(i, carry):
        part = pl.ds(pl.multiple_of(i * 8, 8), 8)
        columns = inlet_cols[part]
        for f in range(NF):
            for t in range(CT):
                shift = (-(f * CT + t)) % cells
                ends[f, t, part] = pltpu.roll(columns, shift, 1) if shift else columns
        return carry

    lax.fori_loop(0, span_len // 8, spread, 0)

    coefs = [[[inv_step * jac[f, d, g] for g in range(NF)] for f in range(NF)] for d in range(3)]
    axial = lax.broadcasted_iota(jnp.int32, (ROWS, cells), 1)
    at_first = axial == 0
    at_last = axial == cells - 1

    def advance(q, halo, target, pad, t, s, first):
        part = pl.ds(pl.multiple_of(PAD + s, 8), ROWS)
        plain = pl.ds(pl.multiple_of(s, 8), ROWS)
        now, diffs, sums = [], [], []
        for g in range(NF):
            c = q[g, t, part]
            if isinstance(t, int) and t == CT - 1:
                cu = halo[1, g, plain]
            else:
                cu = q[g, t + 1, part]
            if isinstance(t, int) and t == 0:
                cd = halo[0, g, plain]
            else:
                cd = q[g, t - 1, part]
            su = q[g, t, pl.ds(PAD + 1 + s, ROWS)]
            sd = q[g, t, pl.ds(PAD - 1 + s, ROWS)]
            au = jnp.where(at_last, 0.0, pltpu.roll(c, cells - 1, 1))
            ad = jnp.where(at_first, ends[g, t, plain], pltpu.roll(c, 1, 1))
            now.append(c)
            diffs.append((cu - cd, su - sd, au - ad))
            sums.append((cu + cd) + (su + sd) + (au + ad))
        speed = rate[t, plain]
        for f in range(NF):
            residual = (6.0 * now[f] - sums[f]) * viscosity
            if not first:
                residual = residual + inv_step * (now[f] - q0[f, t, part])
            for d in range(3):
                for g in range(NF):
                    residual = residual + coefs[d][f][g] * diffs[g][d]
            target[f, t, part if pad else plain] = now[f] - speed * residual

    per_chunk = step // ROWS

    def edges(q, halo, target, pad, chunk, first):
        def one(i, carry):
            s = chunk * step + i * ROWS
            advance(q, halo, target, pad, 0, s, first)
            advance(q, halo, target, pad, CT - 1, s, first)
            return carry

        lax.fori_loop(0, per_chunk, one, 0)

    def inner(q, target, pad, first):
        def one(i, carry):
            t = 1 + i // (span_len // ROWS)
            advance(q, None, target, pad, t, i % (span_len // ROWS) * ROWS, first)
            return carry

        lax.fori_loop(0, (CT - 2) * (span_len // ROWS), one, 0)

    for chunk in range(CHUNKS):
        for side in range(2):
            circ_copy(0, chunk, side).wait_recv()
        edges(q0, halo0, q1, True, chunk, True)
        for side in range(2):
            circ_copy(1, chunk, side).start()
    inner(q0, q1, True, True)
    span_send(1, q1)
    span_take(1, q1)
    inner(q1, out, False, False)
    for chunk in range(CHUNKS):
        for side in range(2):
            circ_copy(1, chunk, side).wait_recv()
        edges(q1, halo1, out, False, chunk, False)

    for copy in rotor_copies + panel_copies:
        copy.wait_send()
    for phase in range(2):
        for chunk in range(CHUNKS):
            for side in range(2):
                circ_copy(phase, chunk, side).wait_send()

        @pl.when(me_s < n_span - 1)
        def _():
            span_copy(phase, 0).wait_send()

        @pl.when(me_s > 0)
        def _():
            span_copy(phase, 1).wait_send()


def body(
    n_circ, n_span,
    q_old, pseudo_rate, flux_jacobians, rotor_face, offsets, owners, slots, weight_idx, weight_table,
):
    nf, ct, span_len, cells = q_old.shape
    f32 = jnp.float32
    hbm = pl.BlockSpec(memory_space=pltpu.HBM)
    vmem = pl.BlockSpec(memory_space=pltpu.VMEM)
    smem = pl.BlockSpec(memory_space=pltpu.SMEM)
    dma = pltpu.SemaphoreType.DMA
    padded = pltpu.VMEM((nf, ct, span_len + 2 * PAD, cells), f32)
    block = pltpu.VMEM((nf, ct, span_len, cells), f32)
    halo = pltpu.VMEM((2, nf, span_len, cells), f32)
    return pl.pallas_call(
        functools.partial(kernel, n_circ, n_span),
        out_shape=pltpu.VMEM(q_old.shape, f32),
        in_specs=[hbm, hbm, smem, vmem, vmem, smem, smem, smem, smem],
        out_specs=vmem,
        scratch_shapes=[
            padded, padded, pltpu.VMEM((ct, span_len, cells), f32), block, halo, halo,
            pltpu.VMEM((n_circ - 1, nf, ct, span_len), f32),
            pltpu.VMEM((n_span, nf, ct, span_len), f32),
            pltpu.VMEM((n_span - 1, nf, ct, span_len), f32),
            pltpu.VMEM((cells, span_len), f32),
            pltpu.VMEM((span_len, cells), f32),
            pltpu.VMEM((2, 2, nf, ct, cells), f32),
            pltpu.VMEM((2, 2, nf, ct, cells), f32),
            dma((2,)),
            dma((n_circ - 1,)), dma((n_circ - 1,)),
            dma((n_span - 1,)), dma((n_span - 1,)),
            dma((2, CHUNKS, 2)), dma((2, CHUNKS, 2)),
            dma((2, 2)), dma((2, 2)),
        ],
        compiler_params=pltpu.CompilerParams(
            collective_id=0, has_side_effects=True, vmem_limit_bytes=56 * 1024 * 1024
        ),
    )(
        q_old, pseudo_rate, flux_jacobians.transpose(1, 0, 2), rotor_face, offsets.reshape(1, span_len),
        owners, slots, weight_idx, weight_table,
    )


def solution(mesh):
    return jax.shard_map(
        functools.partial(body, mesh.shape["circ"], mesh.shape["span"]),
        mesh=mesh,
        in_specs=(
            P(None, "circ", "span", None),
            P("circ", "span", None),
            P(),
            P(None, "circ", "span"),
            P("span"),
            P("circ", "span", None),
            P("circ", "span", None),
            P("circ", "span", None),
            P(),
        ),
        out_specs=P(None, "circ", "span", None),
        check_vma=False,
    )
```

```python
import functools

import jax
import jax.numpy as jnp
from jax import lax
from jax.experimental import pallas as pl
from jax.experimental.pallas import tpu as pltpu
from jax.sharding import PartitionSpec as P

NF = 5
CT = 4
PANELS = 4
ROWS = 32
CHUNKS = 4
EARLY = 2
PAD = 8

inv_step = 0.5
viscosity = 0.1


def remote(src, dst, send, recv, **device):
    return pltpu.make_async_remote_copy(
        src_ref=src,
        dst_ref=dst,
        send_sem=send,
        recv_sem=recv,
        device_id=device,
        device_id_type=pl.DeviceIdType.MESH,
    )


def kernel(
    n_circ, n_span,
    q_hbm, rate_hbm, jac, rotor, offsets, owners, slots, weight_idx, table,
    out,
    q0, q1, rate, ends, halo0, halo1,
    rotor_in, given, taken, inlet_rows, inlet_cols, span_out, span_in,
    local_sem, rotor_s, rotor_r, panel_s, panel_r,
    circ_s, circ_r, span_s, span_r, ready,
):
    span_len = q_hbm.shape[2]
    cells = q_hbm.shape[3]
    step = span_len // CHUNKS
    total = n_circ * CT
    me_c = lax.axis_index("circ")
    me_s = lax.axis_index("span")

    load_q = pltpu.make_async_copy(q_hbm, q0.at[:, :, pl.ds(PAD, span_len)], local_sem.at[0])
    load_q.start()
    load_rate = pltpu.make_async_copy(rate_hbm, rate, local_sem.at[1])
    load_rate.start()

    barrier = pltpu.get_barrier_semaphore()
    for off in range(1, n_circ):
        pl.semaphore_signal(
            barrier, inc=1, device_id={"circ": lax.rem(me_c + off, n_circ)},
            device_id_type=pl.DeviceIdType.MESH,
        )
    def tell(sem, peer):
        pl.semaphore_signal(
            sem, inc=1, device_id={"span": peer}, device_id_type=pl.DeviceIdType.MESH
        )

    for peer in range(1, n_span):
        @pl.when(me_s < peer)
        def _():
            tell(barrier, peer)

    pl.semaphore_wait(barrier, n_circ - 1 + me_s)

    up_c = lax.rem(me_c + 1, n_circ)
    down_c = lax.rem(me_c + n_circ - 1, n_circ)

    rotor_copies = []
    for off in range(1, n_circ):
        copy = remote(
            rotor, rotor_in.at[off - 1], rotor_s.at[off - 1], rotor_r.at[off - 1],
            circ=lax.rem(me_c + off, n_circ),
        )
        copy.start()
        rotor_copies.append(copy)

    def circ_copy(phase, chunk, side):
        part = pl.ds(chunk * step, step)
        row = CT - 1 if side == 0 else 0
        if phase == 0:
            src = q_hbm.at[:, row, part]
            dst = halo0.at[side, :, part]
        else:
            src = q1.at[:, row, pl.ds(PAD + chunk * step, step)]
            dst = halo1.at[side, :, part]
        return remote(
            src, dst, circ_s.at[phase, chunk, side], circ_r.at[phase, chunk, side],
            circ=up_c if side == 0 else down_c,
        )

    for chunk in range(EARLY):
        for side in range(2):
            circ_copy(0, chunk, side).start()

    for peer in range(n_span - 1):
        @pl.when(me_s > peer)
        def _():
            tell(ready, peer)

    def span_copy(phase, side):
        return remote(
            span_out.at[phase, side], span_in.at[phase, side],
            span_s.at[phase, side], span_r.at[phase, side],
            span=lax.rem(me_s + (1 if side == 0 else n_span - 1), n_span),
        )

    def span_send(phase, q):
        for f in range(NF):
            for t in range(CT):
                span_out[phase, 0, f, pl.ds(t, 1)] = q[f, t, pl.ds(PAD + span_len - 1, 1)]
                span_out[phase, 1, f, pl.ds(t, 1)] = q[f, t, pl.ds(PAD, 1)]

        @pl.when(me_s < n_span - 1)
        def _():
            span_copy(phase, 0).start()

        @pl.when(me_s > 0)
        def _():
            span_copy(phase, 1).start()

    def span_take(phase, q):
        @pl.when(me_s > 0)
        def _():
            span_copy(phase, 0).wait_recv()

        @pl.when(me_s == 0)
        def _():
            span_in[phase, 0] = jnp.zeros((NF, CT, cells), jnp.float32)

        @pl.when(me_s < n_span - 1)
        def _():
            span_copy(phase, 1).wait_recv()

        @pl.when(me_s == n_span - 1)
        def _():
            span_in[phase, 1] = jnp.zeros((NF, CT, cells), jnp.float32)

        for f in range(NF):
            for t in range(CT):
                q[f, t, pl.ds(PAD - 1, 1)] = span_in[phase, 0, f, pl.ds(t, 1)]
                q[f, t, pl.ds(PAD + span_len, 1)] = span_in[phase, 1, f, pl.ds(t, 1)]

    lane = lax.broadcasted_iota(jnp.int32, (CT, span_len), 1)
    quarter = lane // (span_len // PANELS)
    width = span_len // PANELS
    turned = lax.broadcasted_iota(jnp.int32, (CT, span_len), 0) - offsets[...]
    turned = jnp.where(turned < 0, turned + total, turned)
    spot = (
        lax.broadcasted_iota(jnp.int32, (n_span, span_len), 0) * PANELS
        + lax.broadcasted_iota(jnp.int32, (n_span, span_len), 1) // width
    )
    mixing = []
    for k in range(PANELS):
        mix = jnp.zeros((n_span, span_len), jnp.float32)
        for j in range(owners.shape[2]):
            weight = table[weight_idx[0, k, j]]
            mix = mix + jnp.where(spot == owners[0, k, j] * PANELS + slots[0, k, j], weight, 0.0)
        mixing.append(mix)

    for copy in rotor_copies:
        copy.wait_recv()
    for f in range(NF):
        rotated = jnp.zeros((CT, span_len), jnp.float32)
        for off in range(n_circ):
            for i in range(CT):
                row = rotor[f, pl.ds(i, 1)] if off == 0 else rotor_in[off - 1, f, pl.ds(i, 1)]
                rotated = jnp.where(turned == (i - CT * off) % total, row, rotated)
        rolled = [rotated] + [pltpu.roll(rotated, width * d, 1) for d in range(1, PANELS)]
        tiled = []
        for k in range(PANELS):
            value = rolled[(0 - k) % PANELS]
            for b in range(1, PANELS):
                value = jnp.where(quarter == b, rolled[(b - k) % PANELS], value)
            tiled.append(value)
        for o in range(n_span):
            value = mixing[0][o:o + 1] * tiled[0]
            for k in range(1, PANELS):
                value = value + mixing[k][o:o + 1] * tiled[k]
            given[o, f] = value

    @pl.when(me_s < n_span - 1)
    def _():
        pl.semaphore_wait(ready, n_span - 1 - me_s)

    panel_copies = []
    for off in range(1, n_span):
        peer = lax.rem(me_s + off, n_span)
        copy = remote(
            given.at[peer], taken.at[off - 1], panel_s.at[off - 1], panel_r.at[off - 1], span=peer
        )
        copy.start()
        panel_copies.append(copy)
    for chunk in range(EARLY, CHUNKS):
        for side in range(2):
            circ_copy(0, chunk, side).start()
    load_q.wait()
    span_send(0, q0)
    inlet_rows[...] = jnp.zeros(inlet_rows.shape, jnp.float32)
    load_rate.wait()
    span_take(0, q0)
    for copy in panel_copies:
        copy.wait_recv()
    for f in range(NF):
        value = given[me_s, f]
        for off in range(1, n_span):
            value = value + taken[off - 1, f]
        inlet_rows[pl.ds(f * CT, CT)] = value
    inlet_cols[...] = inlet_rows[...].T

    def spread(i, carry):
        part = pl.ds(pl.multiple_of(i * 8, 8), 8)
        columns = inlet_cols[part]
        for f in range(NF):
            for t in range(CT):
                shift = (-(f * CT + t)) % cells
                ends[f, t, part] = pltpu.roll(columns, shift, 1) if shift else columns
        return carry

    lax.fori_loop(0, span_len // 8, spread, 0)

    coefs = [[[inv_step * jac[f, d, g] for g in range(NF)] for f in range(NF)] for d in range(3)]
    axial = lax.broadcasted_iota(jnp.int32, (ROWS, cells), 1)
    at_first = axial == 0
    at_last = axial == cells - 1

    def advance(q, halo, target, pad, t, s, first):
        part = pl.ds(pl.multiple_of(PAD + s, 8), ROWS)
        plain = pl.ds(pl.multiple_of(s, 8), ROWS)
        now, diffs, sums = [], [], []
        for g in range(NF):
            c = q[g, t, part]
            if isinstance(t, int) and t == CT - 1:
                cu = halo[1, g, plain]
            else:
                cu = q[g, t + 1, part]
            if isinstance(t, int) and t == 0:
                cd = halo[0, g, plain]
            else:
                cd = q[g, t - 1, part]
            su = q[g, t, pl.ds(PAD + 1 + s, ROWS)]
            sd = q[g, t, pl.ds(PAD - 1 + s, ROWS)]
            au = jnp.where(at_last, 0.0, pltpu.roll(c, cells - 1, 1))
            ad = jnp.where(at_first, ends[g, t, plain], pltpu.roll(c, 1, 1))
            now.append(c)
            diffs.append((cu - cd, su - sd, au - ad))
            sums.append((cu + cd) + (su + sd) + (au + ad))
        speed = rate[t, plain]
        for f in range(NF):
            residual = (6.0 * now[f] - sums[f]) * viscosity
            if not first:
                residual = residual + inv_step * (now[f] - q0[f, t, part])
            for d in range(3):
                for g in range(NF):
                    residual = residual + coefs[d][f][g] * diffs[g][d]
            target[f, t, part if pad else plain] = now[f] - speed * residual

    per_chunk = step // ROWS

    def edges(q, halo, target, pad, chunk, first):
        def one(i, carry):
            s = chunk * step + i * ROWS
            advance(q, halo, target, pad, 0, s, first)
            advance(q, halo, target, pad, CT - 1, s, first)
            return carry

        lax.fori_loop(0, per_chunk, one, 0)

    def inner(q, target, pad, first):
        def one(i, carry):
            t = 1 + i // (span_len // ROWS)
            advance(q, None, target, pad, t, i % (span_len // ROWS) * ROWS, first)
            return carry

        lax.fori_loop(0, (CT - 2) * (span_len // ROWS), one, 0)

    for chunk in range(CHUNKS):
        for side in range(2):
            circ_copy(0, chunk, side).wait_recv()
        edges(q0, halo0, q1, True, chunk, True)
        for side in range(2):
            circ_copy(1, chunk, side).start()
    inner(q0, q1, True, True)
    span_send(1, q1)
    span_take(1, q1)
    inner(q1, out, False, False)
    for chunk in range(CHUNKS):
        for side in range(2):
            circ_copy(1, chunk, side).wait_recv()
        edges(q1, halo1, out, False, chunk, False)

    for copy in rotor_copies + panel_copies:
        copy.wait_send()
    for phase in range(2):
        for chunk in range(CHUNKS):
            for side in range(2):
                circ_copy(phase, chunk, side).wait_send()

        @pl.when(me_s < n_span - 1)
        def _():
            span_copy(phase, 0).wait_send()

        @pl.when(me_s > 0)
        def _():
            span_copy(phase, 1).wait_send()


def body(
    n_circ, n_span,
    q_old, pseudo_rate, flux_jacobians, rotor_face, offsets, owners, slots, weight_idx, weight_table,
):
    nf, ct, span_len, cells = q_old.shape
    f32 = jnp.float32
    hbm = pl.BlockSpec(memory_space=pltpu.HBM)
    vmem = pl.BlockSpec(memory_space=pltpu.VMEM)
    smem = pl.BlockSpec(memory_space=pltpu.SMEM)
    dma = pltpu.SemaphoreType.DMA
    padded = pltpu.VMEM((nf, ct, span_len + 2 * PAD, cells), f32)
    block = pltpu.VMEM((nf, ct, span_len, cells), f32)
    halo = pltpu.VMEM((2, nf, span_len, cells), f32)
    return pl.pallas_call(
        functools.partial(kernel, n_circ, n_span),
        out_shape=pltpu.VMEM(q_old.shape, f32),
        in_specs=[hbm, hbm, smem, vmem, vmem, smem, smem, smem, smem],
        out_specs=vmem,
        scratch_shapes=[
            padded, padded, pltpu.VMEM((ct, span_len, cells), f32), block, halo, halo,
            pltpu.VMEM((n_circ - 1, nf, ct, span_len), f32),
            pltpu.VMEM((n_span, nf, ct, span_len), f32),
            pltpu.VMEM((n_span - 1, nf, ct, span_len), f32),
            pltpu.VMEM((cells, span_len), f32),
            pltpu.VMEM((span_len, cells), f32),
            pltpu.VMEM((2, 2, nf, ct, cells), f32),
            pltpu.VMEM((2, 2, nf, ct, cells), f32),
            dma((2,)),
            dma((n_circ - 1,)), dma((n_circ - 1,)),
            dma((n_span - 1,)), dma((n_span - 1,)),
            dma((2, CHUNKS, 2)), dma((2, CHUNKS, 2)),
            dma((2, 2)), dma((2, 2)), pltpu.SemaphoreType.REGULAR,
        ],
        compiler_params=pltpu.CompilerParams(
            collective_id=0, has_side_effects=True, vmem_limit_bytes=56 * 1024 * 1024
        ),
    )(
        q_old, pseudo_rate, flux_jacobians.transpose(1, 0, 2), rotor_face, offsets.reshape(1, span_len),
        owners, slots, weight_idx, weight_table,
    )


def solution(mesh):
    return jax.shard_map(
        functools.partial(body, mesh.shape["circ"], mesh.shape["span"]),
        mesh=mesh,
        in_specs=(
            P(None, "circ", "span", None),
            P("circ", "span", None),
            P(),
            P(None, "circ", "span"),
            P("span"),
            P("circ", "span", None),
            P("circ", "span", None),
            P("circ", "span", None),
            P(),
        ),
        out_specs=P(None, "circ", "span", None),
        check_vma=False,
    )
```
